256 devices in a mesh: dp: 64 (over z, x, core), tensor: 4 (over y).
Axes of the slice: x: 4, y: 4, z: 8, core: 2. Of those that a mesh axis runs over, the one named last changes fastest.
Arguments:
- rollouts: bfloat16 [24576, 9216], P('dp', 'tensor'), may hold values from -6 to 6
- send_order: int32 [64, 64], P('dp'), may hold values from 0 to 63, each once within a row
- segment_ids: int32 [64, 224], P('dp'), may hold values from 0 to 63, as said below
- offsets: int32 [64, 64], P('dp'), may hold values from 0 to 223, as said below
- ln_gain: float32 [9216], replicated, may hold values from 0.1 to 1.9
- qkv_weight: bfloat16 [9216, 3072], P('dp', 'tensor'), may hold values from -127 to 127, as said below
- qkv_scale: float32 [3072], P('tensor'), may hold values from 6.979167e-05 to 0.0022395833
- out_weight: bfloat16 [1536, 9216], P('tensor', 'dp'), may hold values from -127 to 127, as said below
- out_scale: float32 [9216], P('tensor'), may hold values from 0.00025005208 to 0.0009951052
Outputs:
- block_output: bfloat16 [14336, 9216], P('dp', 'tensor')
The draws below stay inside these ranges and needn't reach their ends.
Inputs may be any that keep to these rules, and one draw needn't show every extreme that they name: `send_order`: each row is an ordering of the 64 responses of one owner. `segment_ids`: on every packed shard the 224 positions form 64 runs of consecutive positions, one for each received slot, each of 1 to 6 tokens; some run of every shard holds exactly 6. offsets[p, s] is the first position of slot s's run on packed shard p; the last run of every shard is one token long. `qkv_weight`: whole numbers. `out_weight`: whole numbers.
All inputs are finite; a program needn't handle non-finite values.
Results may differ from the reference program's by a relative error of at most 0.012.
The reference program's roundings to bfloat16 on the way (of `packed`, `normed`, `projected`, `weights` and `attended`) count: a program that leaves them out, or rounds other values in their place, can miss the bound.
Values may be sent and summed in bfloat16 or wider, within the bound.
No kernel may reach another device: no remote copies, remote signals or barrier semaphores. Data moves between devices by JAX's collectives and lax.ppermute only.
A program may use at most 128 MiB of HBM per device.

```python
import math
import jax
import jax.numpy as jnp
from jax import lax

D = 9216
HEAD = 192
GROUP = 2
MAXLEN = 6
RESP = 64
TOK_DEV = 224
TOKENS = 14336
ROLL_ROWS = 24576
KV_HEADS = 4
HEADS = 8
QKV_COLS = 3072
N_DP = 64


def packing_plan(key):
    folded = jax.random.fold_in(key, 101)
    key_len, key_top, key_slot, key_place = jax.random.split(folded, 4)
    half_count = RESP // 2
    leading = jax.random.randint(key_len, (N_DP, half_count), 1, MAXLEN + 1)
    forced = jax.random.randint(key_top, (N_DP, 1), 0, half_count)
    leading = jnp.where(jnp.arange(half_count)[None, :] == forced, MAXLEN, leading)
    paired = jnp.concatenate([leading, MAXLEN + 1 - leading], axis=1)
    shuffle = jax.vmap(lambda subkey: jax.random.permutation(subkey, RESP))(jax.random.split(key_slot, N_DP))
    lengths = jnp.take_along_axis(paired, shuffle, axis=1)
    placing = jax.vmap(lambda subkey: jax.random.permutation(subkey, RESP))(jax.random.split(key_place, N_DP))
    ordered = jnp.take_along_axis(lengths, placing, axis=1)
    single = jnp.argmax((ordered == 1).astype(jnp.int32), axis=1)[:, None]
    slot_index = jnp.arange(RESP)[None, :]
    last_slot = RESP - 1
    source_index = jnp.where(slot_index == single, last_slot, jnp.where(slot_index == last_slot, single, slot_index))
    placing = jnp.take_along_axis(placing, source_index, axis=1)
    ordered = jnp.take_along_axis(lengths, placing, axis=1)
    starts = jnp.cumsum(ordered, axis=1) - ordered
    offsets = jnp.take_along_axis(starts, jnp.argsort(placing, axis=1), axis=1)
    positions = jnp.arange(TOK_DEV)
    run_index = jnp.sum(starts[:, None, :] <= positions[None, :, None], axis=2) - 1
    segment = jnp.take_along_axis(placing, run_index, axis=1)
    return (segment.astype(jnp.int32), offsets.astype(jnp.int32))


def draw_segment_ids(key, part):
    return packing_plan(key)[0]


def draw_offsets(key, part):
    return packing_plan(key)[1]


def draw_qkv_weight(key, part):
    key = jax.random.fold_in(key, 11)
    return jax.random.randint(key, (D, QKV_COLS), -127, 128).astype(jnp.float32).astype(jnp.bfloat16)


def draw_out_weight(key, part):
    key = jax.random.fold_in(key, 12)
    return jax.random.randint(key, (HEADS * HEAD, D), -127, 128).astype(jnp.float32).astype(jnp.bfloat16)


def draw_qkv_scale(key, part):
    key = jax.random.fold_in(key, 13)
    spread = jax.random.uniform(key, (QKV_COLS,), jnp.float32)
    scales = 0.0067 * float(D) ** (-0.5) * jnp.exp(spread * math.log(4.0))
    return scales.astype(jnp.float32)


def block_levels(key, dims, shards, low, top_value):
    level = 1.0
    for position, parts in shards:
        draws = jax.random.uniform(jax.random.fold_in(jax.random.fold_in(key, 6), position), (parts,), jnp.float32, low / len(shards), top_value / len(shards))
        level = level * jnp.repeat(jnp.exp(draws), dims[position] // parts).reshape((-1,) + (1,) * (len(dims) - 1 - position))
    return level


def centred(stream_key, extent, deviation, bound, pieces=(), kind=jnp.bfloat16):
    entries = deviation * jax.random.normal(stream_key, extent, jnp.float32)
    if pieces:
        entries = entries * block_levels(stream_key, extent, pieces, -0.22, 0.18)
    return jnp.clip(entries, -bound, bound).astype(kind)


def setup_inputs(seed: int = 0) -> dict:
    streams_of = jax.random.split(jax.random.key(seed), 10)
    return {
        "rollouts": centred(streams_of[0], (ROLL_ROWS, D), 1.0, 6.0, ((0, 64), (1, 4))),
        "send_order": jax.vmap(lambda own: jax.random.permutation(own, RESP))(jax.random.split(streams_of[1], N_DP)).reshape((N_DP, RESP)).astype(jnp.int32),
        "segment_ids": draw_segment_ids(jax.random.fold_in(streams_of[9], 71), 0),
        "offsets": draw_offsets(jax.random.fold_in(streams_of[9], 71), 0),
        "ln_gain": jnp.clip(1.0 + 0.18 * jax.random.normal(streams_of[4], (D,), jnp.float32), 0.1, 1.9),
        "qkv_weight": draw_qkv_weight(jax.random.fold_in(streams_of[9], 71), 0),
        "qkv_scale": draw_qkv_scale(jax.random.fold_in(streams_of[9], 71), 0),
        "out_weight": draw_out_weight(jax.random.fold_in(streams_of[9], 71), 0),
        "out_scale": jnp.clip(jnp.exp(math.log(0.0009951052) - 1.3811793 * jax.random.uniform(streams_of[8], (D,), jnp.float32) ** block_levels(streams_of[8], (D,), ((0, 4),), -0.2, 0.2)), 0.00025005208, 0.0009951052),
    }


norm_epsilon = 1e-05
masked_score = -1e+30

def layer_norm(rows_float, ln_gain):
    row_mean = lax.optimization_barrier(jnp.mean(rows_float, axis=1, keepdims=True))
    centered = rows_float - row_mean
    row_var = lax.optimization_barrier(jnp.mean(centered * centered, axis=1, keepdims=True))
    return (centered * lax.rsqrt(row_var + norm_epsilon) * ln_gain).astype(jnp.bfloat16)

def reference(rollouts, send_order, segment_ids, offsets, ln_gain, qkv_weight, qkv_scale, out_weight, out_scale):
    per_slot = RESP // N_DP
    owners = rollouts.reshape(N_DP, RESP, MAXLEN, D)
    score_scale = float(HEAD) ** (-0.5)
    positions = jnp.arange(TOK_DEV, dtype=jnp.int32)

    def one_shard(inputs):
        target, segment, starts = inputs
        source = (segment // per_slot).astype(jnp.int32)
        chosen = send_order[source, (target * per_slot + segment % per_slot).astype(jnp.int32)]
        within = jnp.clip(positions - starts[segment], 0, MAXLEN - 1).astype(jnp.int32)
        packed = owners[source, chosen, within]
        rows_float = packed.astype(jnp.float32)
        normed = layer_norm(rows_float, ln_gain)
        projected = jnp.dot(normed, qkv_weight, preferred_element_type=jnp.float32) * qkv_scale
        projected = lax.optimization_barrier(projected.astype(jnp.bfloat16)).astype(jnp.float32)
        projected = projected.reshape(TOK_DEV, KV_HEADS, GROUP + 2, HEAD)
        queries = projected[:, :, :GROUP]
        key_rows = projected[:, :, GROUP]
        value_rows = projected[:, :, GROUP + 1]
        scores = jnp.einsum('tkgd,ukd->kgtu', queries, key_rows) * score_scale
        allowed = (segment[:, None] == segment[None, :]) & (positions[None, :] <= positions[:, None])
        scores = jnp.where(allowed[None, None], scores, masked_score)
        row_peak = lax.optimization_barrier(jnp.max(scores, axis=3, keepdims=True))
        exponent = jnp.exp(scores - row_peak)
        weights = exponent / lax.optimization_barrier(jnp.sum(exponent, axis=3, keepdims=True))
        weights = lax.optimization_barrier(weights.astype(jnp.bfloat16)).astype(jnp.float32)
        attended = jnp.einsum('kgtu,ukd->tkgd', weights, value_rows).astype(jnp.bfloat16)
        attended = attended.reshape(TOK_DEV, HEADS * HEAD)
        branch = jnp.dot(attended, out_weight, preferred_element_type=jnp.float32) * out_scale
        return (rows_float + branch).astype(jnp.bfloat16)
    results = lax.map(one_shard, (jnp.arange(N_DP, dtype=jnp.int32), segment_ids, offsets))
    return results.reshape(TOKENS, D)
```

```python
import jax
import jax.numpy as jnp
from jax import lax
from jax.sharding import Mesh, PartitionSpec as P

HEAD = 192
norm_epsilon = 1e-05
masked_score = -1e30
DP = ("z", "x", "c")


def layer_norm(rows_float, ln_gain):
    row_mean = jnp.mean(rows_float, axis=1, keepdims=True)
    centered = rows_float - row_mean
    row_var = jnp.mean(centered * centered, axis=1, keepdims=True)
    return (centered * lax.rsqrt(row_var + norm_epsilon) * ln_gain).astype(jnp.bfloat16)


def softmax_rows(scores, allowed):
    scores = jnp.where(allowed, scores, masked_score)
    row_peak = jnp.max(scores, axis=1, keepdims=True)
    exponent = jnp.exp(scores - row_peak)
    return (exponent / jnp.sum(exponent, axis=1, keepdims=True)).astype(jnp.bfloat16)


def masked_attention(queries, key_rows, value_rows, segment):
    token_count = queries.shape[0]
    positions = jnp.arange(token_count, dtype=jnp.int32)
    score_scale = float(queries.shape[1]) ** (-0.5)
    scores = (
        jnp.einsum("td,ud->tu", queries, key_rows, preferred_element_type=jnp.float32) * score_scale
    )
    allowed = (segment[:, None] == segment[None, :]) & (positions[None, :] <= positions[:, None])
    weights = softmax_rows(scores, allowed)
    return jnp.dot(weights, value_rows, preferred_element_type=jnp.float32).astype(jnp.bfloat16)


def shift(value, axis, size, step):
    return lax.ppermute(value, axis, [(i, (i + step) % size) for i in range(size)])


def gather_over_y(block, y_size):
    half = block.shape[0] // 2
    below = shift(block, "y", y_size, 1)
    above = shift(block, "y", y_size, -1)
    far_low = shift(below[:half], "y", y_size, 1)
    far_high = shift(above[half:], "y", y_size, -1)
    return block, below, above, jnp.concatenate([far_low, far_high], axis=0)


def per_device(sizes, rollouts, send_order, segment_ids, offsets, ln_gain,
               qkv_weight, qkv_scale, out_weight, out_scale):
    z_size, x_size, c_size, y_size = sizes
    y = lax.axis_index("y")
    per_plane = z_size // y_size
    swap = []
    for z in range(z_size):
        a, b = z // per_plane, z % per_plane
        for k in range(y_size):
            swap.append((z * y_size + k, (k * per_plane + b) * y_size + a))
    out_block = lax.ppermute(out_weight.T, ("z", "y"), swap)
    qkv_full = lax.all_gather(qkv_weight, DP, axis=0, tiled=True)
    out_full = lax.all_gather(out_block, DP, axis=0, tiled=True)

    response_count = send_order.shape[1]
    feature_count = rollouts.shape[1]
    longest = rollouts.shape[0] // response_count
    slot_rows = rollouts.reshape(response_count, longest, feature_count)
    outgoing = jnp.take(slot_rows, send_order[0], axis=0)
    arrived = lax.all_to_all(outgoing, DP, split_axis=0, concat_axis=0, tiled=True)
    segment = segment_ids[0]
    token_count = segment.shape[0]
    within = jnp.clip(
        jnp.arange(token_count, dtype=jnp.int32) - offsets[0][segment], 0, longest - 1
    )
    packed = arrived.reshape(response_count * longest, feature_count)[segment * longest + within]
    own, below, above, far = gather_over_y(packed, y_size)
    gathered = jnp.zeros((token_count, y_size * feature_count), packed.dtype)
    for step, part in ((0, own), (-1, below), (1, above), (2, far)):
        at = ((y + step) % y_size) * feature_count
        gathered = lax.dynamic_update_slice(gathered, part, (0, at))
    normed = layer_norm(gathered.astype(jnp.float32), ln_gain)
    projected = jnp.dot(normed, qkv_full, preferred_element_type=jnp.float32)
    projected = (projected * qkv_scale).astype(jnp.bfloat16)
    head_size = HEAD
    group_count = projected.shape[1] // head_size - 2
    key_rows = projected[:, group_count * head_size : (group_count + 1) * head_size]
    value_rows = projected[:, (group_count + 1) * head_size :]
    outputs = []
    for member in range(group_count):
        queries = projected[:, member * head_size : (member + 1) * head_size]
        outputs.append(masked_attention(queries, key_rows, value_rows, segment))
    attended = jnp.concatenate(outputs, axis=1)
    attended = lax.all_gather(attended, "y", axis=0, tiled=False)
    out_full = out_full.reshape(y_size, feature_count, attended.shape[2])
    branch = 0.0
    for k in range(y_size):
        branch = branch + jnp.einsum(
            "td,fd->tf", attended[k], out_full[k], preferred_element_type=jnp.float32
        )
    return (packed.astype(jnp.float32) + branch * out_scale).astype(jnp.bfloat16)


def solution(mesh):
    chips = Mesh(mesh.devices.reshape(8, 4, 2, 4), ("z", "x", "c", "y"))
    in_specs = (
        P(DP, "y"),
        P(DP, None),
        P(DP, None),
        P(DP, None),
        P(),
        P(DP, "y"),
        P("y"),
        P("y", DP),
        P("y"),
    )

    def body(*args):
        return per_device((8, 4, 2, 4), *args)

    return jax.shard_map(
        body, mesh=chips, in_specs=in_specs, out_specs=P(DP, "y"), check_vma=False
    )
```

```python
import jax
import jax.numpy as jnp
from jax import lax
from jax.sharding import Mesh, PartitionSpec as P

HEAD = 192
norm_epsilon = 1e-05
masked_score = -1e30
DP = ("z", "x", "c")


def layer_norm(rows_float, ln_gain):
    row_mean = jnp.mean(rows_float, axis=1, keepdims=True)
    centered = rows_float - row_mean
    row_var = jnp.mean(centered * centered, axis=1, keepdims=True)
    return (centered * lax.rsqrt(row_var + norm_epsilon) * ln_gain).astype(jnp.bfloat16)


def softmax_rows(scores, allowed):
    scores = jnp.where(allowed, scores, masked_score)
    row_peak = jnp.max(scores, axis=1, keepdims=True)
    exponent = jnp.exp(scores - row_peak)
    return (exponent / jnp.sum(exponent, axis=1, keepdims=True)).astype(jnp.bfloat16)


def masked_attention(queries, key_rows, value_rows, segment):
    token_count = queries.shape[0]
    positions = jnp.arange(token_count, dtype=jnp.int32)
    score_scale = float(queries.shape[1]) ** (-0.5)
    scores = (
        jnp.einsum("td,ud->tu", queries, key_rows, preferred_element_type=jnp.float32) * score_scale
    )
    allowed = (segment[:, None] == segment[None, :]) & (positions[None, :] <= positions[:, None])
    weights = softmax_rows(scores, allowed)
    return jnp.dot(weights, value_rows, preferred_element_type=jnp.float32).astype(jnp.bfloat16)


def shift(value, axis, size, step):
    return lax.ppermute(value, axis, [(i, (i + step) % size) for i in range(size)])


def gather_over_y(block, y_size):
    half = block.shape[0] // 2
    below = shift(block, "y", y_size, 1)
    above = shift(block, "y", y_size, -1)
    far_low = shift(below[:half], "y", y_size, 1)
    far_high = shift(above[half:], "y", y_size, -1)
    return block, below, above, jnp.concatenate([far_low, far_high], axis=0)


def per_device(sizes, rollouts, send_order, segment_ids, offsets, ln_gain,
               qkv_weight, qkv_scale, out_weight, out_scale):
    z_size, x_size, c_size, y_size = sizes
    y = lax.axis_index("y")
    per_plane = z_size // y_size
    swap = []
    for z in range(z_size):
        a, b = z // per_plane, z % per_plane
        for k in range(y_size):
            swap.append((z * y_size + k, (k * per_plane + b) * y_size + a))
    out_block = lax.ppermute(out_weight.T, ("z", "y"), swap)
    qkv_cols = qkv_weight.shape[1]
    both = jnp.concatenate([qkv_weight, out_block], axis=1)
    both = lax.all_gather(both, DP, axis=0, tiled=True)
    qkv_full, out_full = both[:, :qkv_cols], both[:, qkv_cols:]

    response_count = send_order.shape[1]
    feature_count = rollouts.shape[1]
    longest = rollouts.shape[0] // response_count
    segment = segment_ids[0]
    token_count = segment.shape[0]
    within = jnp.clip(
        jnp.arange(token_count, dtype=jnp.int32) - offsets[0][segment], 0, longest - 1
    )
    take_rows = segment * longest + within
    gathered = jnp.zeros((token_count, y_size * feature_count), rollouts.dtype)
    halves = []
    half_count = feature_count // 2
    for half in range(2):
        slot_rows = rollouts[:, half * half_count : (half + 1) * half_count]
        slot_rows = slot_rows.reshape(response_count, longest, half_count)
        outgoing = jnp.take(slot_rows, send_order[0], axis=0)
        arrived = lax.all_to_all(outgoing, DP, split_axis=0, concat_axis=0, tiled=True)
        part = arrived.reshape(response_count * longest, half_count)[take_rows]
        halves.append(part)
        own, below, above, far = gather_over_y(part, y_size)
        for step, piece in ((0, own), (-1, below), (1, above), (2, far)):
            at = ((y + step) % y_size) * feature_count + half * half_count
            gathered = lax.dynamic_update_slice(gathered, piece, (0, at))
    packed = jnp.concatenate(halves, axis=1)
    normed = layer_norm(gathered.astype(jnp.float32), ln_gain)
    projected = jnp.dot(normed, qkv_full, preferred_element_type=jnp.float32)
    projected = (projected * qkv_scale).astype(jnp.bfloat16)
    head_size = HEAD
    group_count = projected.shape[1] // head_size - 2
    key_rows = projected[:, group_count * head_size : (group_count + 1) * head_size]
    value_rows = projected[:, (group_count + 1) * head_size :]
    outputs = []
    for member in range(group_count):
        queries = projected[:, member * head_size : (member + 1) * head_size]
        outputs.append(masked_attention(queries, key_rows, value_rows, segment))
    attended = jnp.concatenate(outputs, axis=1)
    attended = lax.all_gather(attended, "y", axis=0, tiled=False)
    out_full = out_full.reshape(y_size, feature_count, attended.shape[2])
    branch = 0.0
    for k in range(y_size):
        branch = branch + jnp.einsum(
            "td,fd->tf", attended[k], out_full[k], preferred_element_type=jnp.float32
        )
    return (packed.astype(jnp.float32) + branch * out_scale).astype(jnp.bfloat16)


def solution(mesh):
    chips = Mesh(mesh.devices.reshape(8, 4, 2, 4), ("z", "x", "c", "y"))
    in_specs = (
        P(DP, "y"),
        P(DP, None),
        P(DP, None),
        P(DP, None),
        P(),
        P(DP, "y"),
        P("y"),
        P("y", DP),
        P("y"),
    )

    def body(*args):
        return per_device((8, 4, 2, 4), *args)

    return jax.shard_map(
        body, mesh=chips, in_specs=in_specs, out_specs=P(DP, "y"), check_vma=False
    )
```

```python
import jax
import jax.numpy as jnp
from jax import lax
from jax.sharding import Mesh, PartitionSpec as P

HEAD = 192
norm_epsilon = 1e-05
masked_score = -1e30
DP = ("z", "x", "c")


def layer_norm(rows_float, ln_gain):
    row_mean = jnp.mean(rows_float, axis=1, keepdims=True)
    centered = rows_float - row_mean
    row_var = jnp.mean(centered * centered, axis=1, keepdims=True)
    return (centered * lax.rsqrt(row_var + norm_epsilon) * ln_gain).astype(jnp.bfloat16)


def softmax_rows(scores, allowed):
    scores = jnp.where(allowed, scores, masked_score)
    row_peak = jnp.max(scores, axis=1, keepdims=True)
    exponent = jnp.exp(scores - row_peak)
    return (exponent / jnp.sum(exponent, axis=1, keepdims=True)).astype(jnp.bfloat16)


def masked_attention(queries, key_rows, value_rows, segment):
    token_count = queries.shape[0]
    positions = jnp.arange(token_count, dtype=jnp.int32)
    score_scale = float(queries.shape[1]) ** (-0.5)
    scores = (
        jnp.einsum("td,ud->tu", queries, key_rows, preferred_element_type=jnp.float32) * score_scale
    )
    allowed = (segment[:, None] == segment[None, :]) & (positions[None, :] <= positions[:, None])
    weights = softmax_rows(scores, allowed)
    return jnp.dot(weights, value_rows, preferred_element_type=jnp.float32).astype(jnp.bfloat16)


def shift(value, axis, size, step):
    return lax.ppermute(value, axis, [(i, (i + step) % size) for i in range(size)])


def gather_over_y(block, y_size):
    half = block.shape[0] // 2
    below = shift(block, "y", y_size, 1)
    above = shift(block, "y", y_size, -1)
    far_low = shift(below[:half], "y", y_size, 1)
    far_high = shift(above[half:], "y", y_size, -1)
    return block, below, above, jnp.concatenate([far_low, far_high], axis=0)


def gather_rows(block, z_size, x_size, c_size):
    x, c = lax.axis_index("x"), lax.axis_index("c")
    rows, cols = block.shape
    column = lax.all_gather(block, ("z", "c"), axis=0, tiled=True)
    column = column.reshape(z_size, c_size * rows, cols)
    part = z_size // c_size
    mine = lax.dynamic_slice_in_dim(column, c * part, part, axis=0)
    below = shift(mine, "x", x_size, 1)
    above = shift(mine, "x", x_size, -1)
    mid = part // 2
    far = jnp.concatenate(
        [shift(below[:mid], "x", x_size, 1), shift(above[mid:], "x", x_size, -1)], axis=0
    )
    full = jnp.zeros((z_size, x_size, c_size * rows, cols), block.dtype)
    full = lax.dynamic_update_slice(full, column[:, None], (0, x, 0, 0))
    for step, piece in ((-1, below), (1, above), (2, far)):
        at = (x + step) % x_size
        other = shift(piece, "c", c_size, 1)
        full = lax.dynamic_update_slice(full, piece[:, None], (c * part, at, 0, 0))
        full = lax.dynamic_update_slice(full, other[:, None], ((1 - c) * part, at, 0, 0))
    return full.reshape(z_size * x_size * c_size * rows, cols)


def per_device(sizes, rollouts, send_order, segment_ids, offsets, ln_gain,
               qkv_weight, qkv_scale, out_weight, out_scale):
    z_size, x_size, c_size, y_size = sizes
    y = lax.axis_index("y")
    per_plane = z_size // y_size
    swap = []
    for z in range(z_size):
        a, b = z // per_plane, z % per_plane
        for k in range(y_size):
            swap.append((z * y_size + k, (k * per_plane + b) * y_size + a))
    out_block = lax.ppermute(out_weight.T, ("z", "y"), swap)
    qkv_full = gather_rows(qkv_weight, z_size, x_size, c_size)
    out_full = lax.all_gather(out_block, DP, axis=0, tiled=True)

    response_count = send_order.shape[1]
    feature_count = rollouts.shape[1]
    longest = rollouts.shape[0] // response_count
    segment = segment_ids[0]
    token_count = segment.shape[0]
    within = jnp.clip(
        jnp.arange(token_count, dtype=jnp.int32) - offsets[0][segment], 0, longest - 1
    )
    take_rows = segment * longest + within
    gathered = jnp.zeros((token_count, y_size * feature_count), rollouts.dtype)
    halves = []
    half_count = feature_count // 2
    for half in range(2):
        slot_rows = rollouts[:, half * half_count : (half + 1) * half_count]
        slot_rows = slot_rows.reshape(response_count, longest // 2, 2, half_count)
        outgoing = jnp.take(slot_rows, send_order[0], axis=0, mode="clip")
        arrived = lax.all_to_all(outgoing, DP, split_axis=0, concat_axis=0, tiled=True)
        part = arrived.reshape(response_count * longest, half_count)[take_rows]
        halves.append(part)
        own, below, above, far = gather_over_y(part, y_size)
        for step, piece in ((0, own), (-1, below), (1, above), (2, far)):
            at = ((y + step) % y_size) * feature_count + half * half_count
            gathered = lax.dynamic_update_slice(gathered, piece, (0, at))
    packed = jnp.concatenate(halves, axis=1)
    normed = layer_norm(gathered.astype(jnp.float32), ln_gain)
    projected = jnp.dot(normed, qkv_full, preferred_element_type=jnp.float32)
    projected = (projected * qkv_scale).astype(jnp.bfloat16)
    head_size = HEAD
    group_count = projected.shape[1] // head_size - 2
    key_rows = projected[:, group_count * head_size : (group_count + 1) * head_size]
    value_rows = projected[:, (group_count + 1) * head_size :]
    outputs = []
    for member in range(group_count):
        queries = projected[:, member * head_size : (member + 1) * head_size]
        outputs.append(masked_attention(queries, key_rows, value_rows, segment))
    attended = jnp.concatenate(outputs, axis=1)
    everyone = jnp.zeros((y_size,) + attended.shape, attended.dtype)
    for step in range(y_size):
        piece = shift(attended, "y", y_size, step) if step else attended
        everyone = lax.dynamic_update_slice(everyone, piece[None], ((y - step) % y_size, 0, 0))
    attended = everyone
    out_full = out_full.reshape(y_size, feature_count, attended.shape[2])
    branch = 0.0
    for k in range(y_size):
        branch = branch + jnp.einsum(
            "td,fd->tf", attended[k], out_full[k], preferred_element_type=jnp.float32
        )
    return (packed.astype(jnp.float32) + branch * out_scale).astype(jnp.bfloat16)


def solution(mesh):
    chips = Mesh(mesh.devices.reshape(8, 4, 2, 4), ("z", "x", "c", "y"))
    in_specs = (
        P(DP, "y"),
        P(DP, None),
        P(DP, None),
        P(DP, None),
        P(),
        P(DP, "y"),
        P("y"),
        P("y", DP),
        P("y"),
    )

    def body(*args):
        return per_device((8, 4, 2, 4), *args)

    return jax.shard_map(
        body, mesh=chips, in_specs=in_specs, out_specs=P(DP, "y"), check_vma=False
    )
```

```python
import functools

import jax
import jax.numpy as jnp
from jax import lax
from jax.experimental import pallas as pl
from jax.experimental.pallas import tpu as pltpu
from jax.sharding import Mesh, PartitionSpec as P

HEAD = 192
norm_epsilon = 1e-05
masked_score = -1e30
DP = ("z", "x", "c")


def shift(value, axis, size, step):
    return lax.ppermute(value, axis, [(i, (i + step) % size) for i in range(size)])


def spread(value, axis, size):
    pairs = []
    for i in range(size):
        pairs.append((i * 2, (i + 1) % size * 2))
        pairs.append((i * 2 + 1, (i - 1) % size * 2 + 1))
    return lax.ppermute(value, (axis, "c"), pairs)


def swap_cores(value):
    return lax.ppermute(value, "c", [(0, 1), (1, 0)])


def pick(c, first, second):
    return jnp.where(c == 0, first, second)


def gather_column(block, z_size):
    z, c = lax.axis_index("z"), lax.axis_index("c")
    rows = block.shape[0]
    other = swap_cores(block)
    own = jnp.concatenate([pick(c, block, other), pick(c, other, block)], axis=0)
    mine, theirs = [], []
    held = own
    for _ in range(z_size // 2 - 1):
        held = spread(held, "z", z_size)
        mine.append(held)
        theirs.append(swap_cores(held))
    last = spread(lax.dynamic_slice_in_dim(held, c * rows, rows, axis=0), "z", z_size)
    last_other = swap_cores(last)
    far = jnp.concatenate([pick(c, last, last_other), pick(c, last_other, last)], axis=0)
    stack = jnp.stack([own] + mine + theirs + [far])
    away = jnp.mod(jnp.arange(z_size, dtype=jnp.int32) - z, z_size)
    half = z_size // 2
    ahead = pick(c, half - 1 + away, away)
    behind = pick(c, z_size - away, half - 1 + z_size - away)
    at = jnp.where(away < half, ahead, behind)
    at = jnp.where(away == 0, 0, jnp.where(away == half, z_size - 1, at))
    return jnp.take(stack, at, axis=0, mode="clip")


def gather_over_y(block, y_size):
    half = block.shape[0] // 2
    below = shift(block, "y", y_size, 1)
    above = shift(block, "y", y_size, -1)
    far_low = shift(below[:half], "y", y_size, 1)
    far_high = shift(above[half:], "y", y_size, -1)
    return [[block], [below], [above], [far_low, far_high]]


STEPS = (0, -1, 1, 2)


def piece_stats(parts):
    sums, squares = [], []
    for part in parts:
        rows = part.astype(jnp.float32)
        mean = jnp.mean(rows, axis=1, keepdims=True)
        centered = rows - mean
        sums.append(mean)
        squares.append(jnp.sum(centered * centered, axis=1, keepdims=True))
    return jnp.concatenate(sums, axis=0), jnp.concatenate(squares, axis=0)


def project_kernel(sizes, pos_ref, *refs):
    x_size, y_size = sizes
    pieces = refs[:10]
    (mean_ref, rstd_ref, gain_ref, scale_ref, seg_col_ref, seg_row_ref) = refs[10:16]
    weight_refs = refs[16:21]
    out_ref, weight, normed, sems = refs[21:]
    x, y, c = pos_ref[0], pos_ref[1], pos_ref[2]
    sign = 1 - 2 * c
    part = weight.shape[0] // 2
    spots = (
        weight.at[:, x],
        weight.at[:, lax.rem(x - sign + x_size, x_size)],
        weight.at[:, lax.rem(x + sign + x_size, x_size)],
        weight.at[pl.ds(c * part, part), lax.rem(x + 2, x_size)],
        weight.at[pl.ds((1 - c) * part, part), lax.rem(x + 2, x_size)],
    )
    copies = [
        pltpu.make_async_copy(src, dst, sems.at[i])
        for i, (src, dst) in enumerate(zip(weight_refs, spots))
    ]
    for copy in copies:
        copy.start()
    columns = pieces[0].shape[1]
    index = 0
    for half in range(2):
        for step in STEPS:
            owner = lax.rem(y + step + y_size, y_size)
            gain = gain_ref[owner * 2 + half]
            row = 0
            for _ in range(2 if step == 2 else 1):
                piece = pieces[index]
                index += 1
                count = piece.shape[0]
                rows = pl.ds(row, count)
                value = (piece[...].astype(jnp.float32) - mean_ref[rows, :]) * rstd_ref[rows, :]
                value = (value * gain).astype(jnp.bfloat16)
                normed[owner, rows, half * columns : (half + 1) * columns] = value
                row += count
    for copy in copies:
        copy.wait()
    total = None
    for owner in range(y_size):
        block = weight[2 * owner : 2 * owner + 2]
        block = block.reshape(-1, block.shape[-1])
        term = jnp.dot(normed[owner], block, preferred_element_type=jnp.float32)
        total = term if total is None else total + term
    projected = (total * scale_ref[...]).astype(jnp.bfloat16)
    tokens = projected.shape[0]
    allowed = seg_col_ref[...] == seg_row_ref[...]
    earlier = lax.broadcasted_iota(jnp.int32, (tokens, tokens), 1) <= lax.broadcasted_iota(
        jnp.int32, (tokens, tokens), 0
    )
    allowed = jnp.logical_and(allowed, earlier)
    heads = projected.shape[1] // HEAD - 2
    keys = projected[:, heads * HEAD : (heads + 1) * HEAD]
    values = projected[:, (heads + 1) * HEAD :]
    outs = []
    for head in range(heads):
        queries = projected[:, head * HEAD : (head + 1) * HEAD]
        scores = lax.dot_general(
            queries, keys, (((1,), (1,)), ((), ())), preferred_element_type=jnp.float32
        )
        scores = jnp.where(allowed, scores * float(HEAD) ** (-0.5), masked_score)
        peak = jnp.max(scores, axis=1, keepdims=True)
        exponent = jnp.exp(scores - peak)
        weights = (exponent / jnp.sum(exponent, axis=1, keepdims=True)).astype(jnp.bfloat16)
        outs.append(jnp.dot(weights, values, preferred_element_type=jnp.float32))
    out_ref[...] = jnp.concatenate(outs, axis=1).astype(jnp.bfloat16)


def project_and_attend(sizes, pos, pieces, mean, rstd, gain, scale, segment, weights):
    _, y_size = sizes
    tokens = segment.shape[0]
    z_size, rows, cols = weights[0].shape
    x_size = sizes[0]
    features = pieces[0].shape[1] * 2
    vmem = pl.BlockSpec(memory_space=pltpu.VMEM)
    anywhere = pl.BlockSpec(memory_space=pl.ANY)
    return pl.pallas_call(
        functools.partial(project_kernel, sizes),
        out_shape=jax.ShapeDtypeStruct((tokens, cols - 2 * HEAD), jnp.bfloat16),
        in_specs=[pl.BlockSpec(memory_space=pltpu.SMEM)]
        + [vmem] * (len(pieces) + 6)
        + [anywhere] * len(weights),
        out_specs=vmem,
        scratch_shapes=[
            pltpu.VMEM((z_size, x_size, rows, cols), jnp.bfloat16),
            pltpu.VMEM((y_size, tokens, features), jnp.bfloat16),
            pltpu.SemaphoreType.DMA((len(weights),)),
        ],
        compiler_params=pltpu.CompilerParams(vmem_limit_bytes=44 * 2**20),
        cost_estimate=pl.CostEstimate(
            flops=2 * tokens * features * y_size * cols,
            bytes_accessed=2 * features * y_size * (cols + tokens),
            transcendentals=2 * tokens * tokens,
        ),
    )(pos, *pieces, mean, rstd, gain, scale, segment[:, None], segment[None, :], *weights)


def output_kernel(pos_ref, own, below, above, far, w0, w1, w2, w3, packed_ref, scale_ref, out_ref):
    total = None
    for att, weight in ((own, w0), (below, w1), (above, w2), (far, w3)):
        term = lax.dot_general(
            att[...], weight[0], (((1,), (1,)), ((), ())), preferred_element_type=jnp.float32
        )
        total = term if total is None else total + term
    out_ref[...] = (packed_ref[...].astype(jnp.float32) + total * scale_ref[...]).astype(
        jnp.bfloat16
    )


def project_out(pos, attended, weight, packed, scale):
    tokens, features = packed.shape
    y_size, _, depth = weight.shape
    block = 384
    whole = pl.BlockSpec((tokens, depth), lambda n, p: (0, 0))

    def weight_spec(step):
        return pl.BlockSpec(
            (1, block, depth), lambda n, p: (lax.rem(p[1] + step + y_size, y_size), n, 0)
        )

    return pl.pallas_call(
        output_kernel,
        out_shape=jax.ShapeDtypeStruct((tokens, features), jnp.bfloat16),
        grid_spec=pltpu.PrefetchScalarGridSpec(
            num_scalar_prefetch=1,
            grid=(features // block,),
            in_specs=[whole] * 4
            + [weight_spec(step) for step in STEPS]
            + [
                pl.BlockSpec((tokens, block), lambda n, p: (0, n)),
                pl.BlockSpec((1, block), lambda n, p: (0, n)),
            ],
            out_specs=pl.BlockSpec((tokens, block), lambda n, p: (0, n)),
        ),
        compiler_params=pltpu.CompilerParams(vmem_limit_bytes=24 * 2**20),
        cost_estimate=pl.CostEstimate(
            flops=2 * tokens * features * y_size * depth,
            bytes_accessed=2 * y_size * features * depth,
            transcendentals=0,
        ),
    )(pos, *attended, weight, weight, weight, weight, packed, scale)


def per_device(sizes, rollouts, send_order, segment_ids, offsets, ln_gain,
               qkv_weight, qkv_scale, out_weight, out_scale):
    z_size, x_size, c_size, y_size = sizes
    x, y, c = lax.axis_index("x"), lax.axis_index("y"), lax.axis_index("c")
    pos = jnp.stack([x, y, c]).astype(jnp.int32)
    per_plane = z_size // y_size
    swap = []
    for z in range(z_size):
        a, b = z // per_plane, z % per_plane
        for k in range(y_size):
            swap.append((z * y_size + k, (k * per_plane + b) * y_size + a))
    out_block = lax.ppermute(out_weight.T, ("z", "y"), swap)
    out_full = lax.all_gather(out_block, DP, axis=0, tiled=True)

    column = gather_column(qkv_weight, z_size)
    near = spread(column, "x", x_size)
    near_other = swap_cores(near)
    part = z_size // 2
    far = spread(lax.dynamic_slice_in_dim(near, c * part, part, axis=0), "x", x_size)
    far_other = swap_cores(far)

    response_count = send_order.shape[1]
    feature_count = rollouts.shape[1]
    longest = rollouts.shape[0] // response_count
    segment = segment_ids[0]
    token_count = segment.shape[0]
    within = jnp.clip(
        jnp.arange(token_count, dtype=jnp.int32) - offsets[0][segment], 0, longest - 1
    )
    take_rows = segment * longest + within
    halves, pieces, stats = [], [], []
    half_count = feature_count // 2
    for half in range(2):
        slot_rows = rollouts[:, half * half_count : (half + 1) * half_count]
        slot_rows = slot_rows.reshape(response_count, longest // 2, 2, half_count)
        outgoing = jnp.take(slot_rows, send_order[0], axis=0, mode="clip")
        arrived = lax.all_to_all(outgoing, DP, split_axis=0, concat_axis=0, tiled=True)
        part_rows = arrived.reshape(response_count * longest, half_count)
        part_rows = jnp.take(part_rows, take_rows, axis=0, mode="clip")
        halves.append(part_rows)
        for parts in gather_over_y(part_rows, y_size):
            pieces.extend(parts)
            stats.append(piece_stats(parts))
    packed = jnp.concatenate(halves, axis=1)
    total_count = y_size * feature_count
    mean = sum(m for m, _ in stats) / len(stats)
    spread_sum = sum(s + half_count * (m - mean) * (m - mean) for m, s in stats)
    rstd = lax.rsqrt(spread_sum / total_count + norm_epsilon)

    attended = project_and_attend(
        (x_size, y_size), pos, pieces, mean, rstd,
        ln_gain.reshape(2 * y_size, 1, half_count), qkv_scale[None, :], segment,
        (column, near, near_other, far, far_other),
    )
    around = [attended] + [shift(attended, "y", y_size, step) for step in (1, -1, 2)]
    weight = out_full.reshape(y_size, feature_count, attended.shape[1])
    return project_out(pos, around, weight, packed, out_scale[None, :])


def solution(mesh):
    chips = Mesh(mesh.devices.reshape(8, 4, 2, 4), ("z", "x", "c", "y"))
    in_specs = (
        P(DP, "y"),
        P(DP, None),
        P(DP, None),
        P(DP, None),
        P(),
        P(DP, "y"),
        P("y"),
        P("y", DP),
        P("y"),
    )

    def body(*args):
        return per_device((8, 4, 2, 4), *args)

    return jax.shard_map(
        body, mesh=chips, in_specs=in_specs, out_specs=P(DP, "y"), check_vma=False
    )
```

```python
import functools

import jax
import jax.numpy as jnp
from jax import lax
from jax.experimental import pallas as pl
from jax.experimental.pallas import tpu as pltpu
from jax.sharding import Mesh, PartitionSpec as P

HEAD = 192
norm_epsilon = 1e-05
masked_score = -1e30
DP = ("z", "x", "c")


def shift(value, axis, size, step):
    return lax.ppermute(value, axis, [(i, (i + step) % size) for i in range(size)])


STEPS = (0, -1, 1, 2)


def normalize_kernel(y_size, pos_ref, *refs):
    pieces, gain_ref, out_ref = refs[:10], refs[10], refs[11]
    y = pos_ref[1]
    widths = (pieces[0].shape[1], pieces[5].shape[1])
    starts = (0, widths[0])
    mid = pieces[3].shape[0]
    block = 16
    total_count = y_size * sum(widths)
    owners = [lax.rem(y + step + y_size, y_size) for step in STEPS]
    gains = [
        gain_ref[owner, :, pl.ds(starts[half], widths[half])]
        for half in range(2)
        for owner in owners
    ]

    for side in range(2):
        def step(i, carry, side=side):
            near_rows = pl.ds(pl.multiple_of(side * mid + i * block, block), block)
            far_rows = pl.ds(pl.multiple_of(i * block, block), block)
            views = []
            for half in range(2):
                own, below, above, low, high = pieces[5 * half : 5 * half + 5]
                views += [(own, near_rows), (below, near_rows), (above, near_rows)]
                views += [((low, high)[side], far_rows)]
            total = 0.0
            for ref, rows in views:
                total = total + jnp.sum(ref[rows, :].astype(jnp.float32), axis=1, keepdims=True)
            mean = total / total_count
            total = 0.0
            for ref, rows in views:
                centered = ref[rows, :].astype(jnp.float32) - mean
                total = total + jnp.sum(centered * centered, axis=1, keepdims=True)
            rstd = lax.rsqrt(total / total_count + norm_epsilon)
            for at, (ref, rows) in enumerate(views):
                half, owner = at // 4, owners[at % 4]
                value = (ref[rows, :].astype(jnp.float32) - mean) * rstd * gains[at]
                out_ref[owner, near_rows, pl.ds(starts[half], widths[half])] = value.astype(
                    jnp.bfloat16
                )
            return carry

        lax.fori_loop(0, mid // block, step, 0)


def normalize(y_size, pos, pieces, gain):
    tokens = pieces[0].shape[0]
    columns = pieces[0].shape[1] + pieces[5].shape[1]
    vmem = pl.BlockSpec(memory_space=pltpu.VMEM)
    return pl.pallas_call(
        functools.partial(normalize_kernel, y_size),
        out_shape=jax.ShapeDtypeStruct((y_size, tokens, columns), jnp.bfloat16),
        in_specs=[pl.BlockSpec(memory_space=pltpu.SMEM)] + [vmem] * (len(pieces) + 1),
        out_specs=vmem,
        compiler_params=pltpu.CompilerParams(vmem_limit_bytes=24 * 2**20),
        cost_estimate=pl.CostEstimate(
            flops=20 * tokens * y_size * columns,
            bytes_accessed=8 * tokens * y_size * columns,
            transcendentals=tokens,
        ),
    )(pos, *pieces, gain)


def project_kernel(normed_ref, weight_ref, scale_ref, seg_col_ref, seg_row_ref, out_ref, weight, sems):
    chunks = sems.shape[0]
    y_size, _, features = normed_ref.shape
    per_owner = chunks // y_size
    depth = features // per_owner
    cols = weight.shape[1]
    copies = []
    for i in range(chunks):
        rows = pl.ds(i * depth, depth)
        copies.append(
            pltpu.make_async_copy(
                weight_ref.at[rows, pl.ds(0, cols)], weight.at[rows], sems.at[i]
            )
        )
    for copy in copies:
        copy.start()
    total = None
    for i in range(chunks):
        copies[i].wait()
        at = i % per_owner * depth
        term = jnp.dot(
            normed_ref[i // per_owner][:, at : at + depth],
            weight[i * depth : (i + 1) * depth],
            preferred_element_type=jnp.float32,
        )
        total = term if total is None else total + term
    projected = (total * scale_ref[...]).astype(jnp.bfloat16)
    tokens = projected.shape[0]
    allowed = seg_col_ref[...] == seg_row_ref[...]
    earlier = lax.broadcasted_iota(jnp.int32, (tokens, tokens), 1) <= lax.broadcasted_iota(
        jnp.int32, (tokens, tokens), 0
    )
    allowed = jnp.logical_and(allowed, earlier)
    heads = projected.shape[1] // HEAD - 2
    keys = projected[:, heads * HEAD : (heads + 1) * HEAD]
    values = projected[:, (heads + 1) * HEAD :]
    outs = []
    for head in range(heads):
        queries = projected[:, head * HEAD : (head + 1) * HEAD]
        scores = lax.dot_general(
            queries, keys, (((1,), (1,)), ((), ())), preferred_element_type=jnp.float32
        )
        scores = jnp.where(allowed, scores * float(HEAD) ** (-0.5), masked_score)
        peak = jnp.max(scores, axis=1, keepdims=True)
        exponent = jnp.exp(scores - peak)
        weights = (exponent / jnp.sum(exponent, axis=1, keepdims=True)).astype(jnp.bfloat16)
        outs.append(jnp.dot(weights, values, preferred_element_type=jnp.float32))
    out_ref[...] = jnp.concatenate(outs, axis=1).astype(jnp.bfloat16)


def project_and_attend(normed, weight, scale, segment):
    y_size, tokens, features = normed.shape
    cols = scale.shape[1]
    vmem = pl.BlockSpec(memory_space=pltpu.VMEM)
    return pl.pallas_call(
        project_kernel,
        out_shape=jax.ShapeDtypeStruct((tokens, cols - 2 * HEAD), jnp.bfloat16),
        in_specs=[vmem, pl.BlockSpec(memory_space=pl.ANY), vmem, vmem, vmem],
        out_specs=vmem,
        scratch_shapes=[
            pltpu.VMEM((y_size * features, cols), jnp.bfloat16),
            pltpu.SemaphoreType.DMA((2 * y_size,)),
        ],
        compiler_params=pltpu.CompilerParams(vmem_limit_bytes=56 * 2**20),
        cost_estimate=pl.CostEstimate(
            flops=2 * tokens * features * y_size * cols,
            bytes_accessed=2 * features * y_size * (cols + tokens),
            transcendentals=2 * tokens * tokens,
        ),
    )(normed, weight, scale, segment[:, None], segment[None, :])


def output_kernel(
    blocks, pos_ref, own, below, above, far, w0, w1, w2, w3, packed0, packed1, scale_ref, out_ref
):
    total = None
    for att, weight in ((own, w0), (below, w1), (above, w2), (far, w3)):
        term = lax.dot_general(
            att[...], weight[0], (((1,), (1,)), ((), ())), preferred_element_type=jnp.float32
        )
        total = term if total is None else total + term
    first = pl.program_id(0) < blocks
    packed = jnp.where(first, packed0[...], packed1[...]).astype(jnp.float32)
    out_ref[...] = (packed + total * scale_ref[...]).astype(jnp.bfloat16)


def project_out(pos, attended, weight, packed, scale):
    tokens, columns = packed[0].shape
    features = columns + packed[1].shape[1]
    y_size = weight.shape[0]
    depth = attended[0].shape[1]
    block = 384
    blocks = columns // block
    whole = pl.BlockSpec((tokens, depth), lambda n, p: (0, 0))

    def weight_spec(step):
        return pl.BlockSpec(
            (1, block, depth), lambda n, p: (lax.rem(p[1] + step + y_size, y_size), n, 0)
        )

    return pl.pallas_call(
        functools.partial(output_kernel, blocks),
        out_shape=jax.ShapeDtypeStruct((tokens, features), jnp.bfloat16),
        grid_spec=pltpu.PrefetchScalarGridSpec(
            num_scalar_prefetch=1,
            grid=(features // block,),
            in_specs=[whole] * 4
            + [weight_spec(step) for step in STEPS]
            + [
                pl.BlockSpec((tokens, block), lambda n, p: (0, jnp.minimum(n, blocks - 1))),
                pl.BlockSpec((tokens, block), lambda n, p: (0, jnp.maximum(n - blocks, 0))),
                pl.BlockSpec((1, block), lambda n, p: (0, n)),
            ],
            out_specs=pl.BlockSpec((tokens, block), lambda n, p: (0, n)),
        ),
        compiler_params=pltpu.CompilerParams(vmem_limit_bytes=24 * 2**20),
        cost_estimate=pl.CostEstimate(
            flops=2 * tokens * features * y_size * depth,
            bytes_accessed=2 * y_size * features * depth,
            transcendentals=0,
        ),
    )(pos, *attended, weight, weight, weight, weight, *packed, scale)


def per_device(sizes, rollouts, send_order, segment_ids, offsets, ln_gain,
               qkv_weight, qkv_scale, out_weight, out_scale):
    z_size, x_size, c_size, y_size = sizes
    x, y, c = lax.axis_index("x"), lax.axis_index("y"), lax.axis_index("c")
    pos = jnp.stack([x, y, c]).astype(jnp.int32)
    per_plane = z_size // y_size
    swap = []
    for z in range(z_size):
        a, b = z // per_plane, z % per_plane
        for k in range(y_size):
            swap.append((z * y_size + k, (k * per_plane + b) * y_size + a))
    out_block = lax.ppermute(out_weight.T, ("z", "y"), swap)
    response_count = send_order.shape[1]
    feature_count = rollouts.shape[1]
    longest = rollouts.shape[0] // response_count
    segment = segment_ids[0]
    token_count = segment.shape[0]
    within = jnp.clip(
        jnp.arange(token_count, dtype=jnp.int32) - offsets[0][segment], 0, longest - 1
    )
    take_rows = segment * longest + within
    first = feature_count * 2 // 3
    outgoing = []
    for start, width in ((0, first), (first, feature_count - first)):
        slot_rows = rollouts[:, start : start + width]
        slot_rows = slot_rows.reshape(response_count, longest // 2, 2, width)
        outgoing.append(jnp.take(slot_rows, send_order[0], axis=0, mode="clip"))
    qkv_cols = qkv_weight.shape[1]
    both = jnp.pad(qkv_weight, ((0, 0), (0, out_block.shape[1])))
    outgoing0, outgoing1, both, out_block = lax.optimization_barrier(
        (outgoing[0], outgoing[1], both, out_block)
    )
    both = lax.dynamic_update_slice(both, out_block, (0, qkv_cols))
    both = lax.all_gather(both, DP, axis=0, tiled=True)

    def exchange(block):
        arrived = lax.all_to_all(block, DP, split_axis=0, concat_axis=0, tiled=True)
        arrived = arrived.reshape(response_count * longest, block.shape[3])
        return jnp.take(arrived, take_rows, axis=0, mode="clip")

    mid = token_count // 2
    packed0 = exchange(outgoing0)
    below0, above0 = shift(packed0, "y", y_size, 1), shift(packed0, "y", y_size, -1)
    packed1 = exchange(outgoing1)
    below1, above1 = shift(packed1, "y", y_size, 1), shift(packed1, "y", y_size, -1)
    low0, high0 = shift(below0[:mid], "y", y_size, 1), shift(above0[mid:], "y", y_size, -1)
    low1, high1 = shift(below1[:mid], "y", y_size, 1), shift(above1[mid:], "y", y_size, -1)
    pieces = [packed0, below0, above0, low0, high0, packed1, below1, above1, low1, high1]
    normed = normalize(y_size, pos, pieces, ln_gain.reshape(y_size, 1, feature_count))
    attended = project_and_attend(normed, both, qkv_scale[None, :], segment)
    around = [attended] + [shift(attended, "y", y_size, step) for step in (1, -1, 2)]
    both, around[0] = lax.optimization_barrier((both, around[0]))
    weight = both[:, qkv_cols:].reshape(y_size, feature_count, attended.shape[1])
    return project_out(pos, around, weight, (packed0, packed1), out_scale[None, :])


def solution(mesh):
    chips = Mesh(mesh.devices.reshape(8, 4, 2, 4), ("z", "x", "c", "y"))
    in_specs = (
        P(DP, "y"),
        P(DP, None),
        P(DP, None),
        P(DP, None),
        P(),
        P(DP, "y"),
        P("y"),
        P("y", DP),
        P("y"),
    )

    def body(*args):
        return per_device((8, 4, 2, 4), *args)

    return jax.shard_map(
        body, mesh=chips, in_specs=in_specs, out_specs=P(DP, "y"), check_vma=False
    )
```

```python
import functools

import jax
import jax.numpy as jnp
from jax import lax
from jax.experimental import pallas as pl
from jax.experimental.pallas import tpu as pltpu
from jax.sharding import Mesh, PartitionSpec as P

HEAD = 192
norm_epsilon = 1e-05
masked_score = -1e30
DP = ("z", "x", "c")


def shift(value, axis, size, step):
    return lax.ppermute(value, axis, [(i, (i + step) % size) for i in range(size)])


STEPS = (0, -1, 1, 2)


def normalize_kernel(y_size, pos_ref, *refs):
    pieces, gain_ref, out_ref = refs[:10], refs[10], refs[11]
    y = pos_ref[1]
    widths = (pieces[0].shape[1], pieces[5].shape[1])
    starts = (0, widths[0])
    mid = pieces[3].shape[0]
    block = 16
    total_count = y_size * sum(widths)
    owners = [lax.rem(y + step + y_size, y_size) for step in STEPS]
    gains = [
        gain_ref[owner, :, pl.ds(starts[half], widths[half])]
        for half in range(2)
        for owner in owners
    ]

    for side in range(2):
        def step(i, carry, side=side):
            near_rows = pl.ds(pl.multiple_of(side * mid + i * block, block), block)
            far_rows = pl.ds(pl.multiple_of(i * block, block), block)
            views = []
            for half in range(2):
                own, below, above, low, high = pieces[5 * half : 5 * half + 5]
                views += [(own, near_rows), (below, near_rows), (above, near_rows)]
                views += [((low, high)[side], far_rows)]
            total = 0.0
            for ref, rows in views:
                total = total + jnp.sum(ref[rows, :].astype(jnp.float32), axis=1, keepdims=True)
            mean = total / total_count
            total = 0.0
            for ref, rows in views:
                centered = ref[rows, :].astype(jnp.float32) - mean
                total = total + jnp.sum(centered * centered, axis=1, keepdims=True)
            rstd = lax.rsqrt(total / total_count + norm_epsilon)
            for at, (ref, rows) in enumerate(views):
                half, owner = at // 4, owners[at % 4]
                value = (ref[rows, :].astype(jnp.float32) - mean) * rstd * gains[at]
                out_ref[owner, near_rows, pl.ds(starts[half], widths[half])] = value.astype(
                    jnp.bfloat16
                )
            return carry

        lax.fori_loop(0, mid // block, step, 0)


def normalize(y_size, pos, pieces, gain):
    tokens = pieces[0].shape[0]
    columns = pieces[0].shape[1] + pieces[5].shape[1]
    vmem = pl.BlockSpec(memory_space=pltpu.VMEM)
    return pl.pallas_call(
        functools.partial(normalize_kernel, y_size),
        out_shape=jax.ShapeDtypeStruct((y_size, tokens, columns), jnp.bfloat16),
        in_specs=[pl.BlockSpec(memory_space=pltpu.SMEM)] + [vmem] * (len(pieces) + 1),
        out_specs=vmem,
        compiler_params=pltpu.CompilerParams(vmem_limit_bytes=24 * 2**20),
        cost_estimate=pl.CostEstimate(
            flops=20 * tokens * y_size * columns,
            bytes_accessed=8 * tokens * y_size * columns,
            transcendentals=tokens,
        ),
    )(pos, *pieces, gain)


def project_kernel(normed_ref, weight_ref, scale_ref, seg_col_ref, seg_row_ref, out_ref, weight, sems):
    chunks = sems.shape[0]
    y_size, _, features = normed_ref.shape
    per_owner = chunks // y_size
    depth = features // per_owner
    cols = weight.shape[1]
    copies = []
    for i in range(chunks):
        rows = pl.ds(i * depth, depth)
        copies.append(
            pltpu.make_async_copy(
                weight_ref.at[rows, pl.ds(0, cols)], weight.at[rows], sems.at[i]
            )
        )
    for copy in copies:
        copy.start()
    total = None
    for i in range(chunks):
        copies[i].wait()
        at = i % per_owner * depth
        term = jnp.dot(
            normed_ref[i // per_owner][:, at : at + depth],
            weight[i * depth : (i + 1) * depth],
            preferred_element_type=jnp.float32,
        )
        total = term if total is None else total + term
    projected = (total * scale_ref[...]).astype(jnp.bfloat16)
    tokens = projected.shape[0]
    allowed = seg_col_ref[...] == seg_row_ref[...]
    earlier = lax.broadcasted_iota(jnp.int32, (tokens, tokens), 1) <= lax.broadcasted_iota(
        jnp.int32, (tokens, tokens), 0
    )
    allowed = jnp.logical_and(allowed, earlier)
    heads = projected.shape[1] // HEAD - 2
    keys = projected[:, heads * HEAD : (heads + 1) * HEAD]
    values = projected[:, (heads + 1) * HEAD :]
    outs = []
    for head in range(heads):
        queries = projected[:, head * HEAD : (head + 1) * HEAD]
        scores = lax.dot_general(
            queries, keys, (((1,), (1,)), ((), ())), preferred_element_type=jnp.float32
        )
        scores = jnp.where(allowed, scores * float(HEAD) ** (-0.5), masked_score)
        peak = jnp.max(scores, axis=1, keepdims=True)
        exponent = jnp.exp(scores - peak)
        weights = (exponent / jnp.sum(exponent, axis=1, keepdims=True)).astype(jnp.bfloat16)
        outs.append(jnp.dot(weights, values, preferred_element_type=jnp.float32))
    out_ref[...] = jnp.concatenate(outs, axis=1).astype(jnp.bfloat16)


def project_and_attend(normed, weight, scale, segment):
    y_size, tokens, features = normed.shape
    cols = scale.shape[1]
    vmem = pl.BlockSpec(memory_space=pltpu.VMEM)
    return pl.pallas_call(
        project_kernel,
        out_shape=jax.ShapeDtypeStruct((tokens, cols - 2 * HEAD), jnp.bfloat16),
        in_specs=[vmem, pl.BlockSpec(memory_space=pl.ANY), vmem, vmem, vmem],
        out_specs=vmem,
        scratch_shapes=[
            pltpu.VMEM((y_size * features, cols), jnp.bfloat16),
            pltpu.SemaphoreType.DMA((2 * y_size,)),
        ],
        compiler_params=pltpu.CompilerParams(vmem_limit_bytes=56 * 2**20),
        cost_estimate=pl.CostEstimate(
            flops=2 * tokens * features * y_size * cols,
            bytes_accessed=2 * features * y_size * (cols + tokens),
            transcendentals=2 * tokens * tokens,
        ),
    )(normed, weight, scale, segment[:, None], segment[None, :])


def near_kernel(pos_ref, own, below, above, w0, w1, w2, out_ref):
    total = None
    for att, weight in ((own, w0), (below, w1), (above, w2)):
        term = lax.dot_general(
            att[...], weight[0], (((1,), (1,)), ((), ())), preferred_element_type=jnp.float32
        )
        total = term if total is None else total + term
    out_ref[...] = total


def last_kernel(blocks, pos_ref, low, high, weight, near, packed0, packed1, scale_ref, out_ref):
    far = jnp.concatenate([low[...], high[...]], axis=0)
    total = near[...] + lax.dot_general(
        far, weight[0], (((1,), (1,)), ((), ())), preferred_element_type=jnp.float32
    )
    first = pl.program_id(0) < blocks
    packed = jnp.where(first, packed0[...], packed1[...]).astype(jnp.float32)
    out_ref[...] = (packed + total * scale_ref[...]).astype(jnp.bfloat16)


def out_weight_spec(weight, block, step):
    y_size, _, depth = weight.shape
    return pl.BlockSpec(
        (1, block, depth), lambda n, p: (lax.rem(p[1] + step + y_size, y_size), n, 0)
    )


def project_near(pos, attended, weight):
    tokens, depth = attended[0].shape
    features = weight.shape[1]
    block = 384
    return pl.pallas_call(
        near_kernel,
        out_shape=jax.ShapeDtypeStruct((tokens, features), jnp.float32),
        grid_spec=pltpu.PrefetchScalarGridSpec(
            num_scalar_prefetch=1,
            grid=(features // block,),
            in_specs=[pl.BlockSpec((tokens, depth), lambda n, p: (0, 0))] * 3
            + [out_weight_spec(weight, block, step) for step in STEPS[:3]],
            out_specs=pl.BlockSpec((tokens, block), lambda n, p: (0, n)),
        ),
        compiler_params=pltpu.CompilerParams(vmem_limit_bytes=24 * 2**20),
        cost_estimate=pl.CostEstimate(
            flops=6 * tokens * features * depth, bytes_accessed=6 * features * depth, transcendentals=0
        ),
    )(pos, *attended, weight, weight, weight)


def project_last(pos, low, high, near, weight, packed, scale):
    tokens, features = near.shape
    mid, depth = low.shape
    block = 768
    blocks = packed[0].shape[1] // block
    rows = pl.BlockSpec((mid, depth), lambda n, p: (0, 0))
    return pl.pallas_call(
        functools.partial(last_kernel, blocks),
        out_shape=jax.ShapeDtypeStruct((tokens, features), jnp.bfloat16),
        grid_spec=pltpu.PrefetchScalarGridSpec(
            num_scalar_prefetch=1,
            grid=(features // block,),
            in_specs=[
                rows,
                rows,
                out_weight_spec(weight, block, STEPS[3]),
                pl.BlockSpec((tokens, block), lambda n, p: (0, n)),
                pl.BlockSpec((tokens, block), lambda n, p: (0, jnp.minimum(n, blocks - 1))),
                pl.BlockSpec((tokens, block), lambda n, p: (0, jnp.maximum(n - blocks, 0))),
                pl.BlockSpec((1, block), lambda n, p: (0, n)),
            ],
            out_specs=pl.BlockSpec((tokens, block), lambda n, p: (0, n)),
        ),
        compiler_params=pltpu.CompilerParams(vmem_limit_bytes=24 * 2**20),
        cost_estimate=pl.CostEstimate(
            flops=2 * tokens * features * depth, bytes_accessed=2 * features * depth, transcendentals=0
        ),
    )(pos, low, high, weight, near, *packed, scale)


def per_device(sizes, rollouts, send_order, segment_ids, offsets, ln_gain,
               qkv_weight, qkv_scale, out_weight, out_scale):
    z_size, x_size, c_size, y_size = sizes
    x, y, c = lax.axis_index("x"), lax.axis_index("y"), lax.axis_index("c")
    pos = jnp.stack([x, y, c]).astype(jnp.int32)
    per_plane = z_size // y_size
    swap = []
    for z in range(z_size):
        a, b = z // per_plane, z % per_plane
        for k in range(y_size):
            swap.append((z * y_size + k, (k * per_plane + b) * y_size + a))
    out_block = lax.ppermute(out_weight.T, ("z", "y"), swap)
    response_count = send_order.shape[1]
    feature_count = rollouts.shape[1]
    longest = rollouts.shape[0] // response_count
    segment = segment_ids[0]
    token_count = segment.shape[0]
    within = jnp.clip(
        jnp.arange(token_count, dtype=jnp.int32) - offsets[0][segment], 0, longest - 1
    )
    take_rows = segment * longest + within
    first = feature_count * 2 // 3
    outgoing = []
    for start, width in ((0, first), (first, feature_count - first)):
        slot_rows = rollouts[:, start : start + width]
        slot_rows = slot_rows.reshape(response_count, longest // 2, 2, width)
        outgoing.append(jnp.take(slot_rows, send_order[0], axis=0, mode="clip"))
    qkv_cols = qkv_weight.shape[1]
    both = jnp.pad(qkv_weight, ((0, 0), (0, out_block.shape[1])))
    outgoing0, outgoing1, both, out_block = lax.optimization_barrier(
        (outgoing[0], outgoing[1], both, out_block)
    )
    both = lax.dynamic_update_slice(both, out_block, (0, qkv_cols))
    both = lax.all_gather(both, DP, axis=0, tiled=True)

    def exchange(block):
        arrived = lax.all_to_all(block, DP, split_axis=0, concat_axis=0, tiled=True)
        arrived = arrived.reshape(response_count * longest, block.shape[3])
        return jnp.take(arrived, take_rows, axis=0, mode="clip")

    mid = token_count // 2
    packed0 = exchange(outgoing0)
    below0, above0 = shift(packed0, "y", y_size, 1), shift(packed0, "y", y_size, -1)
    packed1 = exchange(outgoing1)
    below1, above1 = shift(packed1, "y", y_size, 1), shift(packed1, "y", y_size, -1)
    low0, high0 = shift(below0[:mid], "y", y_size, 1), shift(above0[mid:], "y", y_size, -1)
    low1, high1 = shift(below1[:mid], "y", y_size, 1), shift(above1[mid:], "y", y_size, -1)
    pieces = [packed0, below0, above0, low0, high0, packed1, below1, above1, low1, high1]
    normed = normalize(y_size, pos, pieces, ln_gain.reshape(y_size, 1, feature_count))
    attended = project_and_attend(normed, both, qkv_scale[None, :], segment)
    below, above = shift(attended, "y", y_size, 1), shift(attended, "y", y_size, -1)
    low, high = shift(below[:mid], "y", y_size, 1), shift(above[mid:], "y", y_size, -1)
    both, attended = lax.optimization_barrier((both, attended))
    weight = both[:, qkv_cols:].reshape(y_size, feature_count, attended.shape[1])
    near = project_near(pos, (attended, below, above), weight)
    return project_last(pos, low, high, near, weight, (packed0, packed1), out_scale[None, :])


def solution(mesh):
    chips = Mesh(mesh.devices.reshape(8, 4, 2, 4), ("z", "x", "c", "y"))
    in_specs = (
        P(DP, "y"),
        P(DP, None),
        P(DP, None),
        P(DP, None),
        P(),
        P(DP, "y"),
        P("y"),
        P("y", DP),
        P("y"),
    )

    def body(*args):
        return per_device((8, 4, 2, 4), *args)

    return jax.shard_map(
        body, mesh=chips, in_specs=in_specs, out_specs=P(DP, "y"), check_vma=False
    )
```

```python
import functools

import jax
import jax.numpy as jnp
from jax import lax
from jax.experimental import pallas as pl
from jax.experimental.pallas import tpu as pltpu
from jax.sharding import Mesh, PartitionSpec as P

HEAD = 192
norm_epsilon = 1e-05
masked_score = -1e30
DP = ("z", "x", "c")


def shift(value, axis, size, step):
    return lax.ppermute(value, axis, [(i, (i + step) % size) for i in range(size)])


STEPS = (0, -1, 1, 2)


def normalize_kernel(y_size, pos_ref, *refs):
    pieces, gain_ref, out_ref = refs[:10], refs[10], refs[11]
    y = pos_ref[1]
    widths = (pieces[0].shape[1], pieces[5].shape[1])
    starts = (0, widths[0])
    mid = pieces[3].shape[0]
    block = 16
    total_count = y_size * sum(widths)
    owners = [lax.rem(y + step + y_size, y_size) for step in STEPS]
    gains = [
        gain_ref[owner, :, pl.ds(starts[half], widths[half])]
        for half in range(2)
        for owner in owners
    ]

    for side in range(2):
        def step(i, carry, side=side):
            near_rows = pl.ds(pl.multiple_of(side * mid + i * block, block), block)
            far_rows = pl.ds(pl.multiple_of(i * block, block), block)
            views = []
            for half in range(2):
                own, below, above, low, high = pieces[5 * half : 5 * half + 5]
                views += [(own, near_rows), (below, near_rows), (above, near_rows)]
                views += [((low, high)[side], far_rows)]
            total = 0.0
            for ref, rows in views:
                total = total + jnp.sum(ref[rows, :].astype(jnp.float32), axis=1, keepdims=True)
            mean = total / total_count
            total = 0.0
            for ref, rows in views:
                centered = ref[rows, :].astype(jnp.float32) - mean
                total = total + jnp.sum(centered * centered, axis=1, keepdims=True)
            rstd = lax.rsqrt(total / total_count + norm_epsilon)
            for at, (ref, rows) in enumerate(views):
                half, owner = at // 4, owners[at % 4]
                value = (ref[rows, :].astype(jnp.float32) - mean) * rstd * gains[at]
                out_ref[owner, near_rows, pl.ds(starts[half], widths[half])] = value.astype(
                    jnp.bfloat16
                )
            return carry

        lax.fori_loop(0, mid // block, step, 0)


def normalize(y_size, pos, pieces, gain):
    tokens = pieces[0].shape[0]
    columns = pieces[0].shape[1] + pieces[5].shape[1]
    vmem = pl.BlockSpec(memory_space=pltpu.VMEM)
    return pl.pallas_call(
        functools.partial(normalize_kernel, y_size),
        out_shape=jax.ShapeDtypeStruct((y_size, tokens, columns), jnp.bfloat16),
        in_specs=[pl.BlockSpec(memory_space=pltpu.SMEM)] + [vmem] * (len(pieces) + 1),
        out_specs=vmem,
        compiler_params=pltpu.CompilerParams(vmem_limit_bytes=24 * 2**20),
        cost_estimate=pl.CostEstimate(
            flops=20 * tokens * y_size * columns,
            bytes_accessed=8 * tokens * y_size * columns,
            transcendentals=tokens,
        ),
    )(pos, *pieces, gain)


def project_kernel(normed_ref, weight_ref, scale_ref, seg_col_ref, seg_row_ref, out_ref, weight, sems):
    chunks = sems.shape[0]
    y_size, _, features = normed_ref.shape
    per_owner = chunks // y_size
    depth = features // per_owner
    cols = weight.shape[1]
    copies = []
    for i in range(chunks):
        rows = pl.ds(i * depth, depth)
        copies.append(
            pltpu.make_async_copy(
                weight_ref.at[rows, pl.ds(0, cols)], weight.at[rows], sems.at[i]
            )
        )
    for copy in copies:
        copy.start()
    total = None
    for i in range(chunks):
        copies[i].wait()
        at = i % per_owner * depth
        term = jnp.dot(
            normed_ref[i // per_owner][:, at : at + depth],
            weight[i * depth : (i + 1) * depth],
            preferred_element_type=jnp.float32,
        )
        total = term if total is None else total + term
    projected = (total * scale_ref[...]).astype(jnp.bfloat16)
    tokens = projected.shape[0]
    allowed = seg_col_ref[...] == seg_row_ref[...]
    earlier = lax.broadcasted_iota(jnp.int32, (tokens, tokens), 1) <= lax.broadcasted_iota(
        jnp.int32, (tokens, tokens), 0
    )
    allowed = jnp.logical_and(allowed, earlier)
    heads = projected.shape[1] // HEAD - 2
    keys = projected[:, heads * HEAD : (heads + 1) * HEAD]
    values = projected[:, (heads + 1) * HEAD :]
    outs = []
    for head in range(heads):
        queries = projected[:, head * HEAD : (head + 1) * HEAD]
        scores = lax.dot_general(
            queries, keys, (((1,), (1,)), ((), ())), preferred_element_type=jnp.float32
        )
        scores = jnp.where(allowed, scores * float(HEAD) ** (-0.5), masked_score)
        peak = jnp.max(scores, axis=1, keepdims=True)
        exponent = jnp.exp(scores - peak)
        weights = (exponent / jnp.sum(exponent, axis=1, keepdims=True)).astype(jnp.bfloat16)
        outs.append(jnp.dot(weights, values, preferred_element_type=jnp.float32))
    out_ref[...] = jnp.concatenate(outs, axis=1).astype(jnp.bfloat16)


def project_and_attend(normed, weight, scale, segment):
    y_size, tokens, features = normed.shape
    cols = scale.shape[1]
    vmem = pl.BlockSpec(memory_space=pltpu.VMEM)
    return pl.pallas_call(
        project_kernel,
        out_shape=jax.ShapeDtypeStruct((tokens, cols - 2 * HEAD), jnp.bfloat16),
        in_specs=[vmem, pl.BlockSpec(memory_space=pl.ANY), vmem, vmem, vmem],
        out_specs=vmem,
        scratch_shapes=[
            pltpu.VMEM((y_size * features, cols), jnp.bfloat16),
            pltpu.SemaphoreType.DMA((2 * y_size,)),
        ],
        compiler_params=pltpu.CompilerParams(vmem_limit_bytes=56 * 2**20),
        cost_estimate=pl.CostEstimate(
            flops=2 * tokens * features * y_size * cols,
            bytes_accessed=2 * features * y_size * (cols + tokens),
            transcendentals=2 * tokens * tokens,
        ),
    )(normed, weight, scale, segment[:, None], segment[None, :])


def near_kernel(pos_ref, own, below, above, weight, out_ref):
    y_size = weight.shape[0]
    total = None
    for att, step in zip((own, below, above), STEPS):
        term = lax.dot_general(
            att[...],
            weight[lax.rem(pos_ref[1] + step + y_size, y_size)],
            (((1,), (1,)), ((), ())),
            preferred_element_type=jnp.float32,
        )
        total = term if total is None else total + term
    out_ref[...] = total


def last_kernel(pos_ref, low, high, weight, near, packed0, packed1, scale_ref, out_ref):
    y_size = weight.shape[0]
    far = jnp.concatenate([low[...], high[...]], axis=0)
    start = 0
    for packed in (packed0, packed1):
        at = slice(start, start + packed.shape[1])
        start += packed.shape[1]
        total = near[:, at] + lax.dot_general(
            far,
            weight[lax.rem(pos_ref[1] + STEPS[3], y_size), at],
            (((1,), (1,)), ((), ())),
            preferred_element_type=jnp.float32,
        )
        value = packed[...].astype(jnp.float32) + total * scale_ref[:, at]
        out_ref[:, at] = value.astype(jnp.bfloat16)


def on_vmem(kernel, out_shape, flops, pos, *operands):
    vmem = pl.BlockSpec(memory_space=pltpu.VMEM)
    return pl.pallas_call(
        kernel,
        out_shape=out_shape,
        in_specs=[pl.BlockSpec(memory_space=pltpu.SMEM)] + [vmem] * len(operands),
        out_specs=vmem,
        compiler_params=pltpu.CompilerParams(vmem_limit_bytes=24 * 2**20),
        cost_estimate=pl.CostEstimate(flops=flops, bytes_accessed=8 * 2**20, transcendentals=0),
    )(pos, *operands)


def project_near(pos, attended, weight):
    tokens, depth = attended[0].shape
    features = weight.shape[1]
    shape = jax.ShapeDtypeStruct((tokens, features), jnp.float32)
    return on_vmem(near_kernel, shape, 6 * tokens * features * depth, pos, *attended, weight)


def project_last(pos, low, high, near, weight, packed, scale):
    tokens, features = near.shape
    shape = jax.ShapeDtypeStruct((tokens, features), jnp.bfloat16)
    flops = 2 * tokens * features * low.shape[1]
    return on_vmem(last_kernel, shape, flops, pos, low, high, weight, near, *packed, scale)


def per_device(sizes, rollouts, send_order, segment_ids, offsets, ln_gain,
               qkv_weight, qkv_scale, out_weight, out_scale):
    z_size, x_size, c_size, y_size = sizes
    x, y, c = lax.axis_index("x"), lax.axis_index("y"), lax.axis_index("c")
    pos = jnp.stack([x, y, c]).astype(jnp.int32)
    per_plane = z_size // y_size
    swap = []
    for z in range(z_size):
        a, b = z // per_plane, z % per_plane
        for k in range(y_size):
            swap.append((z * y_size + k, (k * per_plane + b) * y_size + a))
    out_block = lax.ppermute(out_weight.T, ("z", "y"), swap)
    response_count = send_order.shape[1]
    feature_count = rollouts.shape[1]
    longest = rollouts.shape[0] // response_count
    segment = segment_ids[0]
    token_count = segment.shape[0]
    within = jnp.clip(
        jnp.arange(token_count, dtype=jnp.int32) - offsets[0][segment], 0, longest - 1
    )
    take_rows = segment * longest + within
    first = feature_count * 2 // 3
    outgoing = []
    for start, width in ((0, first), (first, feature_count - first)):
        slot_rows = rollouts[:, start : start + width]
        slot_rows = slot_rows.reshape(response_count, longest // 2, 2, width)
        outgoing.append(jnp.take(slot_rows, send_order[0], axis=0, mode="clip"))
    qkv_cols = qkv_weight.shape[1]
    both = jnp.pad(qkv_weight, ((0, 0), (0, out_block.shape[1])))
    outgoing0, outgoing1, both, out_block = lax.optimization_barrier(
        (outgoing[0], outgoing[1], both, out_block)
    )
    both = lax.dynamic_update_slice(both, out_block, (0, qkv_cols))
    both = lax.all_gather(both, DP, axis=0, tiled=True)

    def exchange(block):
        arrived = lax.all_to_all(block, DP, split_axis=0, concat_axis=0, tiled=True)
        arrived = arrived.reshape(response_count * longest, block.shape[3])
        return jnp.take(arrived, take_rows, axis=0, mode="clip")

    mid = token_count // 2
    packed0 = exchange(outgoing0)
    below0, above0 = shift(packed0, "y", y_size, 1), shift(packed0, "y", y_size, -1)
    packed1 = exchange(outgoing1)
    below1, above1 = shift(packed1, "y", y_size, 1), shift(packed1, "y", y_size, -1)
    low0, high0 = shift(below0[:mid], "y", y_size, 1), shift(above0[mid:], "y", y_size, -1)
    low1, high1 = shift(below1[:mid], "y", y_size, 1), shift(above1[mid:], "y", y_size, -1)
    pieces = [packed0, below0, above0, low0, high0, packed1, below1, above1, low1, high1]
    normed = normalize(y_size, pos, pieces, ln_gain.reshape(y_size, 1, feature_count))
    attended = project_and_attend(normed, both, qkv_scale[None, :], segment)
    below, above = shift(attended, "y", y_size, 1), shift(attended, "y", y_size, -1)
    low, high = shift(below[:mid], "y", y_size, 1), shift(above[mid:], "y", y_size, -1)
    both, attended = lax.optimization_barrier((both, attended))
    weight = both[:, qkv_cols:].reshape(y_size, feature_count, attended.shape[1])
    near = project_near(pos, (attended, below, above), weight)
    return project_last(pos, low, high, near, weight, (packed0, packed1), out_scale[None, :])


def solution(mesh):
    chips = Mesh(mesh.devices.reshape(8, 4, 2, 4), ("z", "x", "c", "y"))
    in_specs = (
        P(DP, "y"),
        P(DP, None),
        P(DP, None),
        P(DP, None),
        P(),
        P(DP, "y"),
        P("y"),
        P("y", DP),
        P("y"),
    )

    def body(*args):
        return per_device((8, 4, 2, 4), *args)

    return jax.shard_map(
        body, mesh=chips, in_specs=in_specs, out_specs=P(DP, "y"), check_vma=False
    )
```
